32 devices in a mesh: tm: 2 (over x), mesh: 16 (over z, y, core).
Axes of the slice: x: 2, y: 2, z: 4, core: 2. Of those that a mesh axis runs over, the one named last changes fastest.
Arguments:
- prev_ends: float32 [2, 1024, 1024], P('tm', 'mesh'), may hold values from -6 to 6
- initial: float32 [1024, 1024], P('mesh'), may hold values from -6 to 6
- source: float32 [2, 1024, 1024], P(None, 'mesh'), may hold values from -6 to 6
- region: int32 [1024, 1024], P('mesh'), may hold values from 0 to 3
- conductivity: float32 [4], replicated, may hold values from 0.05 to 2
- reluctivity: float32 [4], replicated, may hold values from 0.5 to 2
- saturation: float32 [4], replicated, may hold values from 0.05 to 0.5
Outputs:
- new_ends: float32 [2, 1024, 1024], P('tm', 'mesh')
The draws below stay inside these ranges and needn't reach their ends.
All inputs are finite; a program needn't handle non-finite values.
Results may differ from the reference program's by a relative error of at most 0.0003.
Values sent between devices are 32-bit elements; how exact they have to be, the bound alone decides.
A program may use at most 64 MiB of HBM per device.

```python
import math
import jax
import jax.numpy as jnp
from jax import lax

NY = 1024
FSTEPS = 2
CG_ITERS = 5
REGIONS = 4
SLICES = 2
NX = 1024


def touch_ends(result, rng, low, top_value):
    dims = result.shape
    spot = [jax.random.randint(jax.random.fold_in(rng, axis), (), 0, dims[axis]) for axis in range(len(dims))]
    result = result.at[tuple(spot)].set(low)
    longest = dims.index(max(dims))
    spot[longest] = (spot[longest] + 1) % dims[longest]
    return result.at[tuple(spot)].set(top_value)


def levels(own_key, extent, cuts, low, top_value):
    gain = 1.0
    for position, shards_of in cuts:
        steps = jax.random.uniform(jax.random.fold_in(jax.random.fold_in(own_key, 6), position), (shards_of,), jnp.float32, low / len(cuts), top_value / len(cuts))
        gain = gain * jnp.repeat(jnp.exp(steps), extent[position] // shards_of).reshape((-1,) + (1,) * (len(extent) - 1 - position))
    return gain


def normal_values(own_key, shape, width, most, pieces=(), kind=jnp.bfloat16):
    values = width * jax.random.normal(own_key, shape, jnp.float32)
    if pieces:
        values = values * levels(own_key, shape, pieces, -0.22, 0.18)
    return jnp.clip(values, -most, most).astype(kind)


def setup_inputs(seed: int = 0) -> dict:
    streams_of = jax.random.split(jax.random.key(seed), 8)
    return {
        "prev_ends": normal_values(streams_of[0], (SLICES, NX, NY), 1.0, 6.0, ((0, 2), (1, 16)), jnp.float32),
        "initial": normal_values(streams_of[1], (NX, NY), 1.0, 6.0, ((0, 16),), jnp.float32),
        "source": normal_values(streams_of[2], (2, NX, NY), 1.0, 6.0, ((1, 16),), jnp.float32),
        "region": touch_ends(jax.random.randint(streams_of[3], (NX, NY), 0, REGIONS), jax.random.fold_in(streams_of[3], 1), 0, REGIONS - 1).astype(jnp.int32),
        "conductivity": jnp.clip(jnp.exp(jax.random.uniform(streams_of[4], (REGIONS,), jnp.float32, math.log(0.05), math.log(2.0))), 0.05, 2.0),
        "reluctivity": jnp.clip(jnp.exp(jax.random.uniform(streams_of[5], (REGIONS,), jnp.float32, math.log(0.5), math.log(2.0))), 0.5, 2.0),
        "saturation": jnp.clip(jnp.exp(jax.random.uniform(streams_of[6], (REGIONS,), jnp.float32, math.log(0.05), math.log(0.5))), 0.05, 0.5),
    }


STEP_LENGTH = 1.0
FREQUENCY = 0.1
LUMPED = 0.02


def lookup(region, values_table):
    summed = jnp.zeros(region.shape, values_table.dtype)
    for material in range(REGIONS):
        summed = summed + jnp.where(region == material, values_table[material], jnp.zeros((), values_table.dtype))
    return summed


def reluctance(padded_rows, base_mid, slope_mid):
    padded = jnp.pad(padded_rows, ((0, 0), (1, 1)))
    grad_x = 0.5 * (padded[2:, 1:-1] - padded[:-2, 1:-1])
    grad_y = 0.5 * (padded[1:-1, 2:] - padded[1:-1, :-2])
    return base_mid * (1.0 + slope_mid * (grad_x * grad_x + grad_y * grad_y))


def stiffness(field_pad, weight_pad):
    middle = field_pad[1:-1, 1:-1]
    weight_mid = weight_pad[1:-1, 1:-1]
    summed = jnp.zeros_like(middle)
    cuts = ((slice(None, -2), slice(1, -1)), (slice(2, None), slice(1, -1)), (slice(1, -1), slice(None, -2)), (slice(1, -1), slice(2, None)))
    for rows_cut, cols_cut in cuts:
        edge = 0.5 * (weight_mid + weight_pad[rows_cut, cols_cut])
        summed = summed + edge * (middle - field_pad[rows_cut, cols_cut])
    return summed


def fine_step(field_now, base_pad, slope_pad, conduct_step, current):
    weights = reluctance(jnp.pad(field_now, ((2, 2), (0, 0))), base_pad, slope_pad)
    weight_pad = jnp.pad(weights, ((0, 0), (1, 1)))
    residual = current - stiffness(jnp.pad(field_now, 1), weight_pad)
    iterate = field_now
    direction = residual
    norm_now = jnp.sum(residual * residual)
    for sweep in range(CG_ITERS):
        image = conduct_step * direction + stiffness(jnp.pad(direction, 1), weight_pad)
        step_size = norm_now / jnp.sum(direction * image)
        iterate = iterate + step_size * direction
        residual = residual - step_size * image
        norm_next = jnp.sum(residual * residual)
        direction = residual + (norm_next / norm_now) * direction
        norm_now = norm_next
    return iterate


def reference(prev_ends, initial, source, region, conductivity, reluctivity, saturation):
    conduct = lookup(region, conductivity)
    base = lookup(region, reluctivity)
    slope = lookup(region, saturation)
    base_pad = jnp.pad(base, ((1, 1), (0, 0)))
    slope_pad = jnp.pad(slope, ((1, 1), (0, 0)))
    conduct_step = conduct / STEP_LENGTH
    starts = jnp.concatenate([initial[None], prev_ends[:-1]], axis=0)

    def propagate(packed):
        slice_time, field_now = packed
        for sweep in range(FSTEPS):
            moment = (slice_time * FSTEPS + sweep + 1) * STEP_LENGTH
            current = source[0] * jnp.cos(FREQUENCY * moment) + source[1] * jnp.sin(FREQUENCY * moment)
            field_now = fine_step(field_now, base_pad, slope_pad, conduct_step, current)
        return field_now

    fines = lax.map(propagate, (jnp.arange(SLICES).astype(jnp.float32), starts))
    decay = conduct / (conduct + LUMPED * base)
    corrections = fines - decay * starts

    def chain(carry, correction):
        ended = decay * carry + correction
        return ended, ended

    last_end, new_ends = lax.scan(chain, initial, corrections)
    return new_ends
```

```python
import functools

import jax
import jax.numpy as jnp
from jax import lax
from jax.experimental import pallas as pl
from jax.experimental.pallas import tpu as pltpu
from jax.sharding import PartitionSpec as P

FSTEPS = 2
REGIONS = 4
STEP_LENGTH = 1.0
FREQUENCY = 0.1
LUMPED = 0.02
TILE = 8
HALO = 8
LANES = 128
CHUNKS = 4
MESH = pl.DeviceIdType.MESH
TINY = 3e-7


def folded(product):
    total = product[:, 0:LANES]
    for cut in range(1, product.shape[1] // LANES):
        total = total + product[:, cut * LANES : (cut + 1) * LANES]
    return total


def kernel(
    slices, n,
    prev_ref, initial_ref, source_ref, region_ref, con_tab, rel_tab, sat_tab,
    out_ref,
    u0, u1, reg, src, con, base, slope, wgt, diag, w_s, w_n, w_e, w_w,
    v0, v1, v2, v3, v4, carry, parts,
    local_sem, send_h, recv_h, send_p, recv_p, send_c, recv_c, send_s, recv_s,
):
    t = lax.axis_index("tm")
    m = lax.axis_index("mesh")
    rows, cols = initial_ref.shape
    tall = rows + 2 * HALO
    tiles = tall // TILE
    first, last = m == 0, m == n - 1
    inner = pl.ds(HALO, rows)

    loads = [
        pltpu.make_async_copy(region_ref, reg.at[inner], local_sem.at[0]),
        pltpu.make_async_copy(source_ref, src.at[:, inner], local_sem.at[1]),
    ]
    load_start = pltpu.make_async_copy(initial_ref, u0.at[inner], local_sem.at[2])
    for copy in loads:
        copy.start()

    @pl.when(t == 0)
    def _():
        load_start.start()

    barrier = pltpu.get_barrier_semaphore()
    for hop in range(1, n):
        pl.semaphore_signal(barrier, inc=1, device_id={"mesh": lax.rem(m + hop, n)}, device_id_type=MESH)

    @pl.when(t > 0)
    def _():
        pl.semaphore_signal(barrier, inc=1, device_id={"tm": t - 1}, device_id_type=MESH)

    @pl.when(t < slices - 1)
    def _():
        pl.semaphore_signal(barrier, inc=1, device_id={"tm": t + 1}, device_id_type=MESH)

    def blank(at):
        u0[at, :] = jnp.zeros((HALO, cols), jnp.float32)
        u1[at, :] = jnp.zeros((HALO, cols), jnp.float32)
        src[:, at, :] = jnp.zeros((2, HALO, cols), jnp.float32)
        reg[at, :] = jnp.full((HALO, cols), REGIONS, jnp.int32)

    top, bottom = pl.ds(0, HALO), pl.ds(HALO + rows, HALO)

    @pl.when(first)
    def _():
        blank(top)

    @pl.when(last)
    def _():
        blank(bottom)

    middle = (t > 0) & (t < slices - 1)

    @pl.when(middle)
    def _():
        pl.semaphore_wait(barrier, n + 1)

    @pl.when(jnp.logical_not(middle))
    def _():
        pl.semaphore_wait(barrier, n - 1 + min(slices - 1, 1))

    low, high = pl.ds(0, HALO), pl.ds(rows - HALO, HALO)
    own_low, own_high = pl.ds(HALO, HALO), pl.ds(rows, HALO)

    def halo(slot, up_src, up_dst, down_src, down_dst):
        up = pltpu.make_async_remote_copy(
            src_ref=up_src, dst_ref=up_dst, send_sem=send_h.at[2 * slot], recv_sem=recv_h.at[2 * slot],
            device_id={"mesh": m - 1}, device_id_type=MESH)
        down = pltpu.make_async_remote_copy(
            src_ref=down_src, dst_ref=down_dst, send_sem=send_h.at[2 * slot + 1], recv_sem=recv_h.at[2 * slot + 1],
            device_id={"mesh": m + 1}, device_id_type=MESH)
        return up, down

    halo_reg = halo(0, region_ref.at[low], reg.at[bottom], region_ref.at[high], reg.at[top])
    halo_src = halo(1, source_ref.at[:, low], src.at[:, bottom], source_ref.at[:, high], src.at[:, top])
    halo_first = halo(2, initial_ref.at[low], u0.at[bottom], initial_ref.at[high], u0.at[top])
    halo_later = halo(2, u0.at[own_low], u0.at[bottom], u0.at[own_high], u0.at[top])
    halo_next = halo(3, u1.at[own_low], u1.at[bottom], u1.at[own_high], u1.at[top])

    def start_up(pair):
        @pl.when(m > 0)
        def _():
            pair[0].start()

    def start_down(pair):
        @pl.when(m < n - 1)
        def _():
            pair[1].start()

    def arrive(pair):
        @pl.when(m < n - 1)
        def _():
            pair[0].wait_recv()

        @pl.when(m > 0)
        def _():
            pair[1].wait_recv()

    def sent(pair):
        @pl.when(m > 0)
        def _():
            pair[0].wait_send()

        @pl.when(m < n - 1)
        def _():
            pair[1].wait_send()

    pieces = []
    for k, (offset, length) in enumerate(((0, HALO), (rows - HALO, HALO), (HALO, rows - 2 * HALO))):
        pieces.append(pltpu.make_async_remote_copy(
            src_ref=prev_ref.at[0, pl.ds(offset, length)], dst_ref=u0.at[pl.ds(HALO + offset, length)],
            send_sem=send_p.at[k], recv_sem=recv_p.at[k], device_id={"tm": t + 1}, device_id_type=MESH))

    @pl.when(t < slices - 1)
    def _():
        for piece in pieces:
            piece.start()

    @pl.when(t == 0)
    def _():
        start_up(halo_first)
        start_down(halo_first)

    for pair in (halo_reg, halo_src):
        start_up(pair)
        start_down(pair)

    @pl.when(t > 0)
    def _():
        pieces[0].wait_recv()
        start_up(halo_later)
        pieces[1].wait_recv()
        start_down(halo_later)

    def at(k):
        return pl.ds(pl.multiple_of(k * TILE, TILE), TILE)

    sub = lax.broadcasted_iota(jnp.int32, (TILE, cols), 0)
    lane = lax.broadcasted_iota(jnp.int32, (TILE, cols), 1)

    def around(ref, k):
        here = ref[at(k), :]
        before = ref[at(lax.rem(k + tiles - 1, tiles)), :]
        after = ref[at(lax.rem(k + 1, tiles)), :]
        south = pltpu.roll(jnp.where(sub == 0, after, here), TILE - 1, 0)
        north = pltpu.roll(jnp.where(sub == TILE - 1, before, here), 1, 0)
        east = pltpu.roll(here, cols - 1, 1)
        west = pltpu.roll(here, 1, 1)
        return here, south, north, east, west

    def apply(ref, k):
        here, south, north, east, west = around(ref, k)
        image = (
            diag[at(k), :] * here
            - (w_s[at(k), :] * south + w_n[at(k), :] * north)
            - (w_e[at(k), :] * east + w_w[at(k), :] * west)
        )
        return here, image

    loads[0].wait()
    arrive(halo_reg)

    @pl.loop(0, tiles)
    def _(k):
        kind = reg[at(k), :]
        for table, into in ((con_tab, con), (rel_tab, base), (sat_tab, slope)):
            value = jnp.zeros((TILE, cols), jnp.float32)
            for material in range(REGIONS):
                value = jnp.where(kind == material, table[material], value)
            into[at(k), :] = value

    loads[1].wait()
    arrive(halo_src)

    @pl.when(t == 0)
    def _():
        load_start.wait()

    @pl.when(t > 0)
    def _():
        pieces[2].wait_recv()

    arrive(halo_first)

    def shared(slot, sums):
        for k, partial in enumerate(sums):
            parts[slot, m, k : k + 1, :] = jnp.sum(partial, axis=0, keepdims=True)
        for k in range(len(sums), TILE):
            parts[slot, m, k : k + 1, :] = jnp.zeros((1, LANES), jnp.float32)
        for hop in range(1, n):
            pltpu.make_async_remote_copy(
                src_ref=parts.at[slot, m], dst_ref=parts.at[slot, m],
                send_sem=send_s.at[slot], recv_sem=recv_s.at[slot],
                device_id={"mesh": lax.rem(m + hop, n)}, device_id_type=MESH).start()

    def everyone(slot, sem):
        return pltpu.make_async_copy(
            parts.at[slot, pl.ds(0, n - 1)], parts.at[slot, pl.ds(0, n - 1)], sem.at[slot])

    def gathered(slot, count):
        everyone(slot, recv_s).wait()
        total = parts[slot, 0]
        for other in range(1, n):
            total = total + parts[slot, other]
        summed = jnp.sum(total, axis=1, keepdims=True)
        return [summed[k : k + 1, :] for k in range(count)]

    def owned(k):
        return (k >= HALO // TILE) & (k < tiles - HALO // TILE)

    def zeros(count):
        return tuple(jnp.zeros((TILE, LANES), jnp.float32) for _ in range(count))

    def summed_up(k, sums, products):
        keep = jnp.where(owned(k), 1.0, 0.0)
        return tuple(s + keep * folded(p) for s, p in zip(sums, products))

    def fine_step(sweep, field, finish):
        moment = (t.astype(jnp.float32) * FSTEPS + sweep + 1) * STEP_LENGTH
        angle = jnp.full((1, 1), FREQUENCY * moment, jnp.float32)
        cosine, sine = jnp.cos(angle), jnp.sin(angle)

        @pl.loop(0, tiles)
        def _(k):
            here, south, north, east, west = around(field, k)
            east = jnp.where(lane == cols - 1, 0.0, east)
            west = jnp.where(lane == 0, 0.0, west)
            grad_x = 0.5 * (south - north)
            grad_y = 0.5 * (east - west)
            wgt[at(k), :] = base[at(k), :] * (1.0 + slope[at(k), :] * (grad_x * grad_x + grad_y * grad_y))

        @pl.loop(0, tiles)
        def _(k):
            here, south, north, east, west = around(wgt, k)
            east = 0.5 * (here + jnp.where(lane == cols - 1, 0.0, east))
            west = 0.5 * (here + jnp.where(lane == 0, 0.0, west))
            south = 0.5 * (here + south)
            north = 0.5 * (here + north)
            conduct = con[at(k), :]
            diag[at(k), :] = conduct + (south + north) + (east + west)
            row = m * rows + k * TILE - HALO + sub
            w_s[at(k), :] = jnp.where((row >= 0) & (row < n * rows - 1), south, 0.0)
            w_n[at(k), :] = jnp.where((row >= 1) & (row < n * rows), north, 0.0)
            w_e[at(k), :] = jnp.where(lane == cols - 1, 0.0, east)
            w_w[at(k), :] = jnp.where(lane == 0, 0.0, west)

        def residual(k, sums):
            here, image = apply(field, k)
            current = src[0, at(k), :] * cosine + src[1, at(k), :] * sine
            row = m * rows + k * TILE - HALO + sub
            value = current - (image - con[at(k), :] * here)
            value = jnp.where((row >= 0) & (row < n * rows), value, 0.0)
            v0[at(k), :] = value
            return summed_up(k, sums, (value * value,))

        (m0,) = lax.fori_loop(0, tiles, residual, zeros(1))

        def power_1(k, sums):
            here, image = apply(v0, k)
            v1[at(k), :] = image
            return summed_up(k, sums, (here * image, image * image))

        m1, m2 = lax.fori_loop(0, tiles, power_1, zeros(2))

        def power_2(k, sums):
            here, image = apply(v1, k)
            v2[at(k), :] = image
            return summed_up(k, sums, (here * image,))

        (m3,) = lax.fori_loop(0, tiles, power_2, zeros(1))
        shared(2 * sweep, (m0, m1, m2, m3))

        @pl.loop(0, tiles)
        def _(k):
            v3[at(k), :] = apply(v2, k)[1]

        @pl.loop(0, tiles)
        def _(k):
            v4[at(k), :] = apply(v3, k)[1]

        m0, m1, m2, m3 = gathered(2 * sweep, 4)
        a0 = m0 / m1
        rr1 = a0 * a0 * m2 - m0
        b0 = rr1 / m0
        g0 = 1.0 + b0
        pmp = g0 * g0 * m1 - 2.0 * g0 * a0 * m2 + a0 * a0 * m3
        a1 = rr1 / pmp
        ca = a0 + a1 * g0
        cb = a0 * a1

        def combine(k, sums):
            x1, x2, x3 = v1[at(k), :], v2[at(k), :], v3[at(k), :]
            r0 = v0[at(k), :] - ca * x1 + cb * x2
            r1 = x1 - ca * x2 + cb * x3
            r2 = x2 - ca * x3 + cb * v4[at(k), :]
            v2[at(k), :] = r0
            v3[at(k), :] = r1
            v4[at(k), :] = r2
            return summed_up(k, sums, (r0 * r0, r0 * r1, r1 * r1, r1 * r2, r2 * r2))

        h = lax.fori_loop(0, tiles, combine, zeros(5))

        def power_5(k, sums):
            here, image = apply(v4, k)
            return (sums[0] + folded(here * image),)

        (h5,) = lax.fori_loop(HALO // TILE, tiles - HALO // TILE, power_5, zeros(1))
        shared(2 * sweep + 1, h + (h5,))
        h0, h1, h2, h3, h4, h5 = gathered(2 * sweep + 1, 6)
        i0, i1 = 1.0 / a0, 1.0 / a1
        mix = i1 + b0 * i0
        q0 = -h0 * i1
        q1 = (q0 - h1) * i1
        q2 = (mix * q0 - h1 * i1 - h2) * i1
        f1 = -q0 * i0
        f2 = (-q0 * i0 + h1 * i1 - mix * q0) * i0
        ip, i_m = 1.0 / pmp, 1.0 / m1
        s00 = h1 - q0 * q0 * ip
        s01 = h2 - q0 * q1 * ip
        s02 = h3 - q0 * q2 * ip
        s11 = h3 - q1 * q1 * ip - f1 * f1 * i_m
        s12 = h4 - q1 * q2 * ip - f1 * f2 * i_m
        s22 = h5 - q2 * q2 * ip - f2 * f2 * i_m
        l10, l20 = s01 / s00, s02 / s00
        d1 = s11 - l10 * s01
        e12 = s12 - l10 * s02
        z1 = h1 - l10 * h0
        usable1 = d1 > TINY * h3
        l21 = jnp.where(usable1, e12 / d1, 0.0)
        d2 = s22 - l20 * s02 - l21 * e12
        z2 = h2 - l20 * h0 - l21 * z1
        y2 = jnp.where(usable1 & (d2 > TINY * h5), z2 / d2, 0.0)
        y1 = jnp.where(usable1, z1 / d1, 0.0) - l21 * y2
        y0 = h0 / s00 - l10 * y1 - l20 * y2
        c1 = -(y0 * q0 + y1 * q1 + y2 * q2) * ip
        c0 = -(y1 * f1 + y2 * f2) * i_m
        e0 = ca + c0 + c1 * g0
        e1 = -cb - c1 * a0

        def result(k):
            return (
                field[at(k), :] + (e0 * v0[at(k), :] + e1 * v1[at(k), :])
                + (y0 * v2[at(k), :] + y1 * v3[at(k), :] + y2 * v4[at(k), :])
            )

        finish(result)

    inside = (HALO // TILE, tiles - HALO // TILE)

    def between(result):
        u1[at(inside[0]), :] = result(inside[0])
        start_up(halo_next)
        u1[at(inside[1] - 1), :] = result(inside[1] - 1)
        start_down(halo_next)

        @pl.loop(inside[0] + 1, inside[1] - 1)
        def _(k):
            u1[at(k), :] = result(k)

        arrive(halo_next)

    span = rows // CHUNKS
    onward = [
        pltpu.make_async_remote_copy(
            src_ref=out_ref.at[0, pl.ds(c * span, span)], dst_ref=carry.at[pl.ds(c * span, span)],
            send_sem=send_c.at[c], recv_sem=recv_c.at[c], device_id={"tm": t + 1}, device_id_type=MESH)
        for c in range(CHUNKS)
    ]

    def final(result):
        @pl.when(t > 0)
        def _():
            @pl.loop(0, rows // TILE)
            def _(k):
                up = k + HALO // TILE
                conduct = con[at(up), :]
                decay = conduct / (conduct + LUMPED * base[at(up), :])
                wgt[at(k), :] = decay
                out_ref[0, at(k), :] = result(up) - decay * u0[at(up), :]

        for c in range(CHUNKS):
            @pl.when(t == 0)
            def _():
                @pl.loop(c * span // TILE, (c + 1) * span // TILE)
                def _(k):
                    out_ref[0, at(k), :] = result(k + HALO // TILE)

            @pl.when(t > 0)
            def _():
                onward[c].wait_recv()

                @pl.loop(c * span // TILE, (c + 1) * span // TILE)
                def _(k):
                    out_ref[0, at(k), :] = out_ref[0, at(k), :] + wgt[at(k), :] * carry[at(k), :]

            @pl.when(t < slices - 1)
            def _():
                onward[c].start()

    fine_step(0, u0, between)
    fine_step(1, u1, final)

    for pair in (halo_reg, halo_src, halo_first, halo_next):
        sent(pair)

    @pl.when(t < slices - 1)
    def _():
        for copy in pieces + onward:
            copy.wait_send()

    for slot in range(2 * FSTEPS):
        everyone(slot, send_s).wait()


def shards(slices, n, prev_ends, initial, source, region, conductivity, reluctivity, saturation):
    rows, cols = initial.shape
    tall = rows + 2 * HALO
    grid = pltpu.VMEM((tall, cols), jnp.float32)
    hbm = pl.BlockSpec(memory_space=pl.ANY)
    smem = pl.BlockSpec(memory_space=pltpu.SMEM)
    dma = pltpu.SemaphoreType.DMA
    return pl.pallas_call(
        functools.partial(kernel, slices, n),
        out_shape=jax.ShapeDtypeStruct((1, rows, cols), jnp.float32),
        in_specs=[hbm] * 4 + [smem] * 3,
        out_specs=pl.BlockSpec(memory_space=pltpu.VMEM),
        scratch_shapes=[
            grid, grid, pltpu.VMEM((tall, cols), jnp.int32), pltpu.VMEM((2, tall, cols), jnp.float32),
            *([grid] * 14),
            pltpu.VMEM((rows, cols), jnp.float32),
            pltpu.VMEM((2 * FSTEPS, n, TILE, LANES), jnp.float32),
            dma((3,)), dma((8,)), dma((8,)), dma((3,)), dma((3,)), dma((CHUNKS,)), dma((CHUNKS,)),
            dma((2 * FSTEPS,)), dma((2 * FSTEPS,)),
        ],
        compiler_params=pltpu.CompilerParams(
            collective_id=0, has_side_effects=True, vmem_limit_bytes=32 * 1024 * 1024),
    )(prev_ends, initial, source, region, conductivity, reluctivity, saturation)


def solution(mesh):
    in_specs = (
        P("tm", "mesh", None), P("mesh", None), P(None, "mesh", None), P("mesh", None), P(), P(), P(),
    )
    return jax.shard_map(
        functools.partial(shards, mesh.shape["tm"], mesh.shape["mesh"]),
        mesh=mesh, in_specs=in_specs, out_specs=P("tm", "mesh", None), check_vma=False)
```

```python
import functools

import jax
import jax.numpy as jnp
from jax import lax
from jax.experimental import pallas as pl
from jax.experimental.pallas import tpu as pltpu
from jax.sharding import PartitionSpec as P

FSTEPS = 2
REGIONS = 4
STEP_LENGTH = 1.0
FREQUENCY = 0.1
LUMPED = 0.02
TILE = 8
HALO = 8
LANES = 128
CHUNKS = 4
MESH = pl.DeviceIdType.MESH
TINY = 3e-7


def folded(product):
    total = product[:, 0:LANES]
    for cut in range(1, product.shape[1] // LANES):
        total = total + product[:, cut * LANES : (cut + 1) * LANES]
    return total


def kernel(
    slices, n,
    prev_ref, initial_ref, source_ref, region_ref, con_ref, rel_ref, sat_ref,
    out_ref,
    u0, u1, reg, src, con, base, slope, wgt, diag, w_s, w_n, w_e, w_w,
    v0, v1, v2, v3, v4, carry, parts, con_tab, rel_tab, sat_tab,
    local_sem, send_h, recv_h, send_p, recv_p, send_c, recv_c, send_s, recv_s,
):
    t = lax.axis_index("tm")
    m = lax.axis_index("mesh")
    rows, cols = initial_ref.shape
    tall = rows + 2 * HALO
    tiles = tall // TILE
    first, last = m == 0, m == n - 1
    inner = pl.ds(HALO, rows)

    loads = [
        pltpu.make_async_copy(region_ref, reg.at[inner], local_sem.at[0]),
        pltpu.make_async_copy(source_ref, src.at[:, inner], local_sem.at[1]),
        pltpu.make_async_copy(con_ref, con_tab, local_sem.at[3]),
        pltpu.make_async_copy(rel_ref, rel_tab, local_sem.at[4]),
        pltpu.make_async_copy(sat_ref, sat_tab, local_sem.at[5]),
    ]
    load_start = pltpu.make_async_copy(initial_ref, u0.at[inner], local_sem.at[2])
    for copy in loads:
        copy.start()

    @pl.when(t == 0)
    def _():
        load_start.start()

    barrier = pltpu.get_barrier_semaphore()
    for hop in range(1, n):
        pl.semaphore_signal(barrier, inc=1, device_id={"mesh": lax.rem(m + hop, n)}, device_id_type=MESH)

    @pl.when(t > 0)
    def _():
        pl.semaphore_signal(barrier, inc=1, device_id={"tm": t - 1}, device_id_type=MESH)

    @pl.when(t < slices - 1)
    def _():
        pl.semaphore_signal(barrier, inc=1, device_id={"tm": t + 1}, device_id_type=MESH)

    def blank(at):
        u0[at, :] = jnp.zeros((HALO, cols), jnp.float32)
        u1[at, :] = jnp.zeros((HALO, cols), jnp.float32)
        src[:, at, :] = jnp.zeros((2, HALO, cols), jnp.float32)
        reg[at, :] = jnp.full((HALO, cols), REGIONS, jnp.int32)

    top, bottom = pl.ds(0, HALO), pl.ds(HALO + rows, HALO)

    @pl.when(first)
    def _():
        blank(top)

    @pl.when(last)
    def _():
        blank(bottom)

    middle = (t > 0) & (t < slices - 1)

    @pl.when(middle)
    def _():
        pl.semaphore_wait(barrier, n + 1)

    @pl.when(jnp.logical_not(middle))
    def _():
        pl.semaphore_wait(barrier, n - 1 + min(slices - 1, 1))

    low, high = pl.ds(0, HALO), pl.ds(rows - HALO, HALO)
    own_low, own_high = pl.ds(HALO, HALO), pl.ds(rows, HALO)

    def halo(slot, up_src, up_dst, down_src, down_dst):
        up = pltpu.make_async_remote_copy(
            src_ref=up_src, dst_ref=up_dst, send_sem=send_h.at[2 * slot], recv_sem=recv_h.at[2 * slot],
            device_id={"mesh": m - 1}, device_id_type=MESH)
        down = pltpu.make_async_remote_copy(
            src_ref=down_src, dst_ref=down_dst, send_sem=send_h.at[2 * slot + 1], recv_sem=recv_h.at[2 * slot + 1],
            device_id={"mesh": m + 1}, device_id_type=MESH)
        return up, down

    halo_reg = halo(0, region_ref.at[low], reg.at[bottom], region_ref.at[high], reg.at[top])
    halo_src = halo(1, source_ref.at[:, low], src.at[:, bottom], source_ref.at[:, high], src.at[:, top])
    halo_first = halo(2, initial_ref.at[low], u0.at[bottom], initial_ref.at[high], u0.at[top])
    halo_later = halo(2, u0.at[own_low], u0.at[bottom], u0.at[own_high], u0.at[top])
    halo_next = halo(3, u1.at[own_low], u1.at[bottom], u1.at[own_high], u1.at[top])

    def start_up(pair):
        @pl.when(m > 0)
        def _():
            pair[0].start()

    def start_down(pair):
        @pl.when(m < n - 1)
        def _():
            pair[1].start()

    def arrive(pair):
        @pl.when(m < n - 1)
        def _():
            pair[0].wait_recv()

        @pl.when(m > 0)
        def _():
            pair[1].wait_recv()

    def sent(pair):
        @pl.when(m > 0)
        def _():
            pair[0].wait_send()

        @pl.when(m < n - 1)
        def _():
            pair[1].wait_send()

    pieces = []
    for k, (offset, length) in enumerate(((0, HALO), (rows - HALO, HALO), (HALO, rows - 2 * HALO))):
        pieces.append(pltpu.make_async_remote_copy(
            src_ref=prev_ref.at[0, pl.ds(offset, length)], dst_ref=u0.at[pl.ds(HALO + offset, length)],
            send_sem=send_p.at[k], recv_sem=recv_p.at[k], device_id={"tm": t + 1}, device_id_type=MESH))

    @pl.when(t < slices - 1)
    def _():
        for piece in pieces:
            piece.start()

    @pl.when(t == 0)
    def _():
        start_up(halo_first)
        start_down(halo_first)

    for pair in (halo_reg, halo_src):
        start_up(pair)
        start_down(pair)

    @pl.when(t > 0)
    def _():
        pieces[0].wait_recv()
        start_up(halo_later)
        pieces[1].wait_recv()
        start_down(halo_later)

    def at(k):
        return pl.ds(pl.multiple_of(k * TILE, TILE), TILE)

    sub = lax.broadcasted_iota(jnp.int32, (TILE, cols), 0)
    lane = lax.broadcasted_iota(jnp.int32, (TILE, cols), 1)

    def around(ref, k):
        here = ref[at(k), :]
        before = ref[at(lax.rem(k + tiles - 1, tiles)), :]
        after = ref[at(lax.rem(k + 1, tiles)), :]
        south = pltpu.roll(jnp.where(sub == 0, after, here), TILE - 1, 0)
        north = pltpu.roll(jnp.where(sub == TILE - 1, before, here), 1, 0)
        east = pltpu.roll(here, cols - 1, 1)
        west = pltpu.roll(here, 1, 1)
        return here, south, north, east, west

    def apply(ref, k):
        here, south, north, east, west = around(ref, k)
        image = (
            diag[at(k), :] * here
            - (w_s[at(k), :] * south + w_n[at(k), :] * north)
            - (w_e[at(k), :] * east + w_w[at(k), :] * west)
        )
        return here, image

    loads[0].wait()
    for copy in loads[2:]:
        copy.wait()
    arrive(halo_reg)

    @pl.loop(0, tiles, unroll=10)
    def _(k):
        kind = reg[at(k), :]
        for table, into in ((con_tab, con), (rel_tab, base), (sat_tab, slope)):
            value = jnp.zeros((TILE, cols), jnp.float32)
            for material in range(REGIONS):
                value = jnp.where(kind == material, table[material], value)
            into[at(k), :] = value

    loads[1].wait()
    arrive(halo_src)

    @pl.when(t == 0)
    def _():
        load_start.wait()

    @pl.when(t > 0)
    def _():
        pieces[2].wait_recv()

    arrive(halo_first)

    def shared(slot, sums):
        for k, partial in enumerate(sums):
            parts[slot, m, k : k + 1, :] = jnp.sum(partial, axis=0, keepdims=True)
        for k in range(len(sums), TILE):
            parts[slot, m, k : k + 1, :] = jnp.zeros((1, LANES), jnp.float32)
        for hop in range(1, n):
            pltpu.make_async_remote_copy(
                src_ref=parts.at[slot, m], dst_ref=parts.at[slot, m],
                send_sem=send_s.at[slot], recv_sem=recv_s.at[slot],
                device_id={"mesh": lax.rem(m + hop, n)}, device_id_type=MESH).start()

    def everyone(slot, sem):
        return pltpu.make_async_copy(
            parts.at[slot, pl.ds(0, n - 1)], parts.at[slot, pl.ds(0, n - 1)], sem.at[slot])

    def gathered(slot, count):
        everyone(slot, recv_s).wait()
        total = parts[slot, 0]
        for other in range(1, n):
            total = total + parts[slot, other]
        summed = jnp.sum(total, axis=1, keepdims=True)
        return [summed[k : k + 1, :] for k in range(count)]

    def owned(k):
        return (k >= HALO // TILE) & (k < tiles - HALO // TILE)

    def zeros(count):
        return tuple(jnp.zeros((TILE, LANES), jnp.float32) for _ in range(count))

    def summed_up(k, sums, products):
        keep = jnp.where(owned(k), 1.0, 0.0)
        return tuple(s + keep * folded(p) for s, p in zip(sums, products))

    def fine_step(sweep, field, finish):
        moment = (t.astype(jnp.float32) * FSTEPS + sweep + 1) * STEP_LENGTH
        angle = jnp.full((1, 1), FREQUENCY * moment, jnp.float32)
        cosine, sine = jnp.cos(angle), jnp.sin(angle)

        @pl.loop(0, tiles, unroll=10)
        def _(k):
            here, south, north, east, west = around(field, k)
            east = jnp.where(lane == cols - 1, 0.0, east)
            west = jnp.where(lane == 0, 0.0, west)
            grad_x = 0.5 * (south - north)
            grad_y = 0.5 * (east - west)
            wgt[at(k), :] = base[at(k), :] * (1.0 + slope[at(k), :] * (grad_x * grad_x + grad_y * grad_y))

        @pl.loop(0, tiles, unroll=10)
        def _(k):
            here, south, north, east, west = around(wgt, k)
            east = 0.5 * (here + jnp.where(lane == cols - 1, 0.0, east))
            west = 0.5 * (here + jnp.where(lane == 0, 0.0, west))
            south = 0.5 * (here + south)
            north = 0.5 * (here + north)
            conduct = con[at(k), :]
            diag[at(k), :] = conduct + (south + north) + (east + west)
            row = m * rows + k * TILE - HALO + sub
            w_s[at(k), :] = jnp.where((row >= 0) & (row < n * rows - 1), south, 0.0)
            w_n[at(k), :] = jnp.where((row >= 1) & (row < n * rows), north, 0.0)
            w_e[at(k), :] = jnp.where(lane == cols - 1, 0.0, east)
            w_w[at(k), :] = jnp.where(lane == 0, 0.0, west)

        def residual(k, sums):
            here, image = apply(field, k)
            current = src[0, at(k), :] * cosine + src[1, at(k), :] * sine
            row = m * rows + k * TILE - HALO + sub
            value = current - (image - con[at(k), :] * here)
            value = jnp.where((row >= 0) & (row < n * rows), value, 0.0)
            v0[at(k), :] = value
            return summed_up(k, sums, (value * value,))

        (m0,) = lax.fori_loop(0, tiles, residual, zeros(1), unroll=10)

        def power_1(k, sums):
            here, image = apply(v0, k)
            v1[at(k), :] = image
            return summed_up(k, sums, (here * image, image * image))

        m1, m2 = lax.fori_loop(0, tiles, power_1, zeros(2), unroll=10)

        def power_2(k, sums):
            here, image = apply(v1, k)
            v2[at(k), :] = image
            return summed_up(k, sums, (here * image,))

        (m3,) = lax.fori_loop(0, tiles, power_2, zeros(1), unroll=10)
        shared(2 * sweep, (m0, m1, m2, m3))

        @pl.loop(0, tiles, unroll=10)
        def _(k):
            v3[at(k), :] = apply(v2, k)[1]

        @pl.loop(0, tiles, unroll=10)
        def _(k):
            v4[at(k), :] = apply(v3, k)[1]

        m0, m1, m2, m3 = gathered(2 * sweep, 4)
        a0 = m0 / m1
        rr1 = a0 * a0 * m2 - m0
        b0 = rr1 / m0
        g0 = 1.0 + b0
        pmp = g0 * g0 * m1 - 2.0 * g0 * a0 * m2 + a0 * a0 * m3
        a1 = rr1 / pmp
        ca = a0 + a1 * g0
        cb = a0 * a1

        def combine(k, sums):
            x1, x2, x3 = v1[at(k), :], v2[at(k), :], v3[at(k), :]
            r0 = v0[at(k), :] - ca * x1 + cb * x2
            r1 = x1 - ca * x2 + cb * x3
            r2 = x2 - ca * x3 + cb * v4[at(k), :]
            v2[at(k), :] = r0
            v3[at(k), :] = r1
            v4[at(k), :] = r2
            return summed_up(k, sums, (r0 * r0, r0 * r1, r1 * r1, r1 * r2, r2 * r2))

        h = lax.fori_loop(0, tiles, combine, zeros(5), unroll=10)

        def power_5(k, sums):
            here, image = apply(v4, k)
            return (sums[0] + folded(here * image),)

        (h5,) = lax.fori_loop(HALO // TILE, tiles - HALO // TILE, power_5, zeros(1))
        shared(2 * sweep + 1, h + (h5,))
        h0, h1, h2, h3, h4, h5 = gathered(2 * sweep + 1, 6)
        i0, i1 = 1.0 / a0, 1.0 / a1
        mix = i1 + b0 * i0
        q0 = -h0 * i1
        q1 = (q0 - h1) * i1
        q2 = (mix * q0 - h1 * i1 - h2) * i1
        f1 = -q0 * i0
        f2 = (-q0 * i0 + h1 * i1 - mix * q0) * i0
        ip, i_m = 1.0 / pmp, 1.0 / m1
        s00 = h1 - q0 * q0 * ip
        s01 = h2 - q0 * q1 * ip
        s02 = h3 - q0 * q2 * ip
        s11 = h3 - q1 * q1 * ip - f1 * f1 * i_m
        s12 = h4 - q1 * q2 * ip - f1 * f2 * i_m
        s22 = h5 - q2 * q2 * ip - f2 * f2 * i_m
        l10, l20 = s01 / s00, s02 / s00
        d1 = s11 - l10 * s01
        e12 = s12 - l10 * s02
        z1 = h1 - l10 * h0
        usable1 = d1 > TINY * h3
        l21 = jnp.where(usable1, e12 / d1, 0.0)
        d2 = s22 - l20 * s02 - l21 * e12
        z2 = h2 - l20 * h0 - l21 * z1
        y2 = jnp.where(usable1 & (d2 > TINY * h5), z2 / d2, 0.0)
        y1 = jnp.where(usable1, z1 / d1, 0.0) - l21 * y2
        y0 = h0 / s00 - l10 * y1 - l20 * y2
        c1 = -(y0 * q0 + y1 * q1 + y2 * q2) * ip
        c0 = -(y1 * f1 + y2 * f2) * i_m
        e0 = ca + c0 + c1 * g0
        e1 = -cb - c1 * a0

        def result(k):
            return (
                field[at(k), :] + (e0 * v0[at(k), :] + e1 * v1[at(k), :])
                + (y0 * v2[at(k), :] + y1 * v3[at(k), :] + y2 * v4[at(k), :])
            )

        finish(result)

    inside = (HALO // TILE, tiles - HALO // TILE)

    def between(result):
        u1[at(inside[0]), :] = result(inside[0])
        start_up(halo_next)
        u1[at(inside[1] - 1), :] = result(inside[1] - 1)
        start_down(halo_next)

        @pl.loop(inside[0] + 1, inside[1] - 1)
        def _(k):
            u1[at(k), :] = result(k)

        arrive(halo_next)

    span = rows // CHUNKS
    onward = [
        pltpu.make_async_remote_copy(
            src_ref=out_ref.at[0, pl.ds(c * span, span)], dst_ref=carry.at[pl.ds(c * span, span)],
            send_sem=send_c.at[c], recv_sem=recv_c.at[c], device_id={"tm": t + 1}, device_id_type=MESH)
        for c in range(CHUNKS)
    ]

    def final(result):
        @pl.when(t > 0)
        def _():
            @pl.loop(0, rows // TILE)
            def _(k):
                up = k + HALO // TILE
                conduct = con[at(up), :]
                decay = conduct / (conduct + LUMPED * base[at(up), :])
                wgt[at(k), :] = decay
                out_ref[0, at(k), :] = result(up) - decay * u0[at(up), :]

        for c in range(CHUNKS):
            @pl.when(t == 0)
            def _():
                @pl.loop(c * span // TILE, (c + 1) * span // TILE)
                def _(k):
                    out_ref[0, at(k), :] = result(k + HALO // TILE)

            @pl.when(t > 0)
            def _():
                onward[c].wait_recv()

                @pl.loop(c * span // TILE, (c + 1) * span // TILE)
                def _(k):
                    out_ref[0, at(k), :] = out_ref[0, at(k), :] + wgt[at(k), :] * carry[at(k), :]

            @pl.when(t < slices - 1)
            def _():
                onward[c].start()

    fine_step(0, u0, between)
    fine_step(1, u1, final)

    for pair in (halo_reg, halo_src, halo_first, halo_next):
        sent(pair)

    @pl.when(t < slices - 1)
    def _():
        for copy in pieces + onward:
            copy.wait_send()

    for slot in range(2 * FSTEPS):
        everyone(slot, send_s).wait()


def shards(slices, n, prev_ends, initial, source, region, conductivity, reluctivity, saturation):
    rows, cols = initial.shape
    tall = rows + 2 * HALO
    grid = pltpu.VMEM((tall, cols), jnp.float32)
    hbm = pl.BlockSpec(memory_space=pltpu.HBM)
    dma = pltpu.SemaphoreType.DMA
    return pl.pallas_call(
        functools.partial(kernel, slices, n),
        out_shape=jax.ShapeDtypeStruct((1, rows, cols), jnp.float32),
        in_specs=[hbm] * 7,
        out_specs=pl.BlockSpec(memory_space=pltpu.VMEM),
        scratch_shapes=[
            grid, grid, pltpu.VMEM((tall, cols), jnp.int32), pltpu.VMEM((2, tall, cols), jnp.float32),
            *([grid] * 14),
            pltpu.VMEM((rows, cols), jnp.float32),
            pltpu.VMEM((2 * FSTEPS, n, TILE, LANES), jnp.float32),
            *([pltpu.SMEM((REGIONS,), jnp.float32)] * 3),
            dma((6,)), dma((8,)), dma((8,)), dma((3,)), dma((3,)), dma((CHUNKS,)), dma((CHUNKS,)),
            dma((2 * FSTEPS,)), dma((2 * FSTEPS,)),
        ],
        compiler_params=pltpu.CompilerParams(
            collective_id=0, has_side_effects=True, vmem_limit_bytes=32 * 1024 * 1024),
    )(prev_ends, initial, source, region, conductivity, reluctivity, saturation)


def solution(mesh):
    in_specs = (
        P("tm", "mesh", None), P("mesh", None), P(None, "mesh", None), P("mesh", None), P(), P(), P(),
    )
    return jax.shard_map(
        functools.partial(shards, mesh.shape["tm"], mesh.shape["mesh"]),
        mesh=mesh, in_specs=in_specs, out_specs=P("tm", "mesh", None), check_vma=False)
```

```python
import functools

import jax
import jax.numpy as jnp
from jax import lax
from jax.experimental import pallas as pl
from jax.experimental.pallas import tpu as pltpu
from jax.sharding import PartitionSpec as P

FSTEPS = 2
REGIONS = 4
STEP_LENGTH = 1.0
FREQUENCY = 0.1
LUMPED = 0.02
TILE = 8
HALO = 8
LANES = 128
CHUNKS = 4
MESH = pl.DeviceIdType.MESH
TINY = 3e-7


def folded(product):
    total = product[:, 0:LANES]
    for cut in range(1, product.shape[1] // LANES):
        total = total + product[:, cut * LANES : (cut + 1) * LANES]
    return total


def kernel(
    slices, n,
    prev_ref, initial_ref, source_ref, region_ref, con_ref, rel_ref, sat_ref,
    out_ref,
    u0, u1, reg, src, con, base, slope, wgt, diag, w_s, w_n, w_e, w_w,
    v0, v1, v2, v3, v4, carry, parts, con_tab, rel_tab, sat_tab,
    local_sem, send_h, recv_h, send_p, recv_p, send_c, recv_c, send_s, recv_s,
):
    t = lax.axis_index("tm")
    m = lax.axis_index("mesh")
    rows, cols = initial_ref.shape
    tall = rows + 2 * HALO
    tiles = tall // TILE
    first, last = m == 0, m == n - 1
    inner = pl.ds(HALO, rows)

    loads = [
        pltpu.make_async_copy(region_ref, reg.at[inner], local_sem.at[0]),
        pltpu.make_async_copy(source_ref, src.at[:, inner], local_sem.at[1]),
        pltpu.make_async_copy(con_ref, con_tab, local_sem.at[3]),
        pltpu.make_async_copy(rel_ref, rel_tab, local_sem.at[4]),
        pltpu.make_async_copy(sat_ref, sat_tab, local_sem.at[5]),
    ]
    load_start = pltpu.make_async_copy(initial_ref, u0.at[inner], local_sem.at[2])
    for copy in loads:
        copy.start()

    @pl.when(t == 0)
    def _():
        load_start.start()

    barrier = pltpu.get_barrier_semaphore()
    for hop in range(1, n):
        pl.semaphore_signal(barrier, inc=1, device_id={"mesh": lax.rem(m + hop, n)}, device_id_type=MESH)

    @pl.when(t > 0)
    def _():
        pl.semaphore_signal(barrier, inc=1, device_id={"tm": t - 1}, device_id_type=MESH)

    @pl.when(t < slices - 1)
    def _():
        pl.semaphore_signal(barrier, inc=1, device_id={"tm": t + 1}, device_id_type=MESH)

    def blank(at):
        u0[at, :] = jnp.zeros((HALO, cols), jnp.float32)
        u1[at, :] = jnp.zeros((HALO, cols), jnp.float32)
        src[:, at, :] = jnp.zeros((2, HALO, cols), jnp.float32)
        reg[at, :] = jnp.full((HALO, cols), REGIONS, jnp.int32)

    top, bottom = pl.ds(0, HALO), pl.ds(HALO + rows, HALO)

    @pl.when(first)
    def _():
        blank(top)

    @pl.when(last)
    def _():
        blank(bottom)

    middle = (t > 0) & (t < slices - 1)

    @pl.when(middle)
    def _():
        pl.semaphore_wait(barrier, n + 1)

    @pl.when(jnp.logical_not(middle))
    def _():
        pl.semaphore_wait(barrier, n - 1 + min(slices - 1, 1))

    low, high = pl.ds(0, HALO), pl.ds(rows - HALO, HALO)
    own_low, own_high = pl.ds(HALO, HALO), pl.ds(rows, HALO)

    def halo(slot, up_src, up_dst, down_src, down_dst):
        up = pltpu.make_async_remote_copy(
            src_ref=up_src, dst_ref=up_dst, send_sem=send_h.at[2 * slot], recv_sem=recv_h.at[2 * slot],
            device_id={"mesh": m - 1}, device_id_type=MESH)
        down = pltpu.make_async_remote_copy(
            src_ref=down_src, dst_ref=down_dst, send_sem=send_h.at[2 * slot + 1], recv_sem=recv_h.at[2 * slot + 1],
            device_id={"mesh": m + 1}, device_id_type=MESH)
        return up, down

    halo_reg = halo(0, region_ref.at[low], reg.at[bottom], region_ref.at[high], reg.at[top])
    halo_src = halo(1, source_ref.at[:, low], src.at[:, bottom], source_ref.at[:, high], src.at[:, top])
    halo_first = halo(2, initial_ref.at[low], u0.at[bottom], initial_ref.at[high], u0.at[top])
    halo_later = halo(2, u0.at[own_low], u0.at[bottom], u0.at[own_high], u0.at[top])
    halo_next = halo(3, u1.at[own_low], u1.at[bottom], u1.at[own_high], u1.at[top])

    def start_up(pair):
        @pl.when(m > 0)
        def _():
            pair[0].start()

    def start_down(pair):
        @pl.when(m < n - 1)
        def _():
            pair[1].start()

    def arrive(pair):
        @pl.when(m < n - 1)
        def _():
            pair[0].wait_recv()

        @pl.when(m > 0)
        def _():
            pair[1].wait_recv()

    def sent(pair):
        @pl.when(m > 0)
        def _():
            pair[0].wait_send()

        @pl.when(m < n - 1)
        def _():
            pair[1].wait_send()

    pieces = []
    for k, (offset, length) in enumerate(((0, HALO), (rows - HALO, HALO), (HALO, rows - 2 * HALO))):
        pieces.append(pltpu.make_async_remote_copy(
            src_ref=prev_ref.at[0, pl.ds(offset, length)], dst_ref=u0.at[pl.ds(HALO + offset, length)],
            send_sem=send_p.at[k], recv_sem=recv_p.at[k], device_id={"tm": t + 1}, device_id_type=MESH))

    @pl.when(t < slices - 1)
    def _():
        for piece in pieces:
            piece.start()

    @pl.when(t == 0)
    def _():
        start_up(halo_first)
        start_down(halo_first)

    for pair in (halo_reg, halo_src):
        start_up(pair)
        start_down(pair)

    @pl.when(t > 0)
    def _():
        pieces[0].wait_recv()
        start_up(halo_later)
        pieces[1].wait_recv()
        start_down(halo_later)

    def at(k):
        return pl.ds(pl.multiple_of(k * TILE, TILE), TILE)

    sub = lax.broadcasted_iota(jnp.int32, (TILE, cols), 0)
    lane = lax.broadcasted_iota(jnp.int32, (TILE, cols), 1)

    def around(ref, k):
        here = ref[at(k), :]
        before = ref[at(lax.rem(k + tiles - 1, tiles)), :]
        after = ref[at(lax.rem(k + 1, tiles)), :]
        south = pltpu.roll(jnp.where(sub == 0, after, here), TILE - 1, 0)
        north = pltpu.roll(jnp.where(sub == TILE - 1, before, here), 1, 0)
        east = pltpu.roll(here, cols - 1, 1)
        west = pltpu.roll(here, 1, 1)
        return here, south, north, east, west

    def apply(ref, k):
        here, south, north, east, west = around(ref, k)
        image = (
            diag[at(k), :] * here
            - (w_s[at(k), :] * south + w_n[at(k), :] * north)
            - (w_e[at(k), :] * east + w_w[at(k), :] * west)
        )
        return here, image

    loads[0].wait()
    for copy in loads[2:]:
        copy.wait()
    arrive(halo_reg)

    @pl.loop(0, tiles, unroll=tiles)
    def _(k):
        kind = reg[at(k), :]
        for table, into in ((con_tab, con), (rel_tab, base), (sat_tab, slope)):
            value = jnp.zeros((TILE, cols), jnp.float32)
            for material in range(REGIONS):
                value = jnp.where(kind == material, table[material], value)
            into[at(k), :] = value

    loads[1].wait()

    @pl.when(t == 0)
    def _():
        load_start.wait()

    @pl.when(t > 0)
    def _():
        pieces[2].wait_recv()

    def first_halos():
        arrive(halo_src)
        arrive(halo_first)

    def later_halos():
        arrive(halo_next)

    def shared(slot, sums):
        for k, partial in enumerate(sums):
            parts[slot, m, k : k + 1, :] = jnp.sum(partial, axis=0, keepdims=True)
        for k in range(len(sums), TILE):
            parts[slot, m, k : k + 1, :] = jnp.zeros((1, LANES), jnp.float32)
        for hop in range(1, n):
            pltpu.make_async_remote_copy(
                src_ref=parts.at[slot, m], dst_ref=parts.at[slot, m],
                send_sem=send_s.at[slot], recv_sem=recv_s.at[slot],
                device_id={"mesh": lax.rem(m + hop, n)}, device_id_type=MESH).start()

    def everyone(slot, sem):
        return pltpu.make_async_copy(
            parts.at[slot, pl.ds(0, n - 1)], parts.at[slot, pl.ds(0, n - 1)], sem.at[slot])

    def gathered(slot, count):
        everyone(slot, recv_s).wait()
        total = parts[slot, 0]
        for other in range(1, n):
            total = total + parts[slot, other]
        summed = jnp.sum(total, axis=1, keepdims=True)
        return [summed[k : k + 1, :] for k in range(count)]

    def owned(k):
        return (k >= HALO // TILE) & (k < tiles - HALO // TILE)

    def zeros(count):
        return tuple(jnp.zeros((TILE, LANES), jnp.float32) for _ in range(count))

    def summed_up(k, sums, products):
        keep = jnp.where(owned(k), 1.0, 0.0)
        return tuple(s + keep * folded(p) for s, p in zip(sums, products))

    def fine_step(sweep, field, arrived, idle, finish):
        moment = (t.astype(jnp.float32) * FSTEPS + sweep + 1) * STEP_LENGTH
        angle = jnp.full((1, 1), FREQUENCY * moment, jnp.float32)
        cosine, sine = jnp.cos(angle), jnp.sin(angle)

        def weights(k, sums):
            here, south, north, east, west = around(field, k)
            east = jnp.where(lane == cols - 1, 0.0, east)
            west = jnp.where(lane == 0, 0.0, west)
            grad_x = 0.5 * (south - north)
            grad_y = 0.5 * (east - west)
            wgt[at(k), :] = base[at(k), :] * (1.0 + slope[at(k), :] * (grad_x * grad_x + grad_y * grad_y))
            return sums

        def edges(k, sums):
            here, south, north, east, west = around(wgt, k)
            east = 0.5 * (here + jnp.where(lane == cols - 1, 0.0, east))
            west = 0.5 * (here + jnp.where(lane == 0, 0.0, west))
            south = 0.5 * (here + south)
            north = 0.5 * (here + north)
            conduct = con[at(k), :]
            diag[at(k), :] = conduct + (south + north) + (east + west)
            row = m * rows + k * TILE - HALO + sub
            w_s[at(k), :] = jnp.where((row >= 0) & (row < n * rows - 1), south, 0.0)
            w_n[at(k), :] = jnp.where((row >= 1) & (row < n * rows), north, 0.0)
            w_e[at(k), :] = jnp.where(lane == cols - 1, 0.0, east)
            w_w[at(k), :] = jnp.where(lane == 0, 0.0, west)
            return sums

        def residual(k, sums):
            here, image = apply(field, k)
            current = src[0, at(k), :] * cosine + src[1, at(k), :] * sine
            row = m * rows + k * TILE - HALO + sub
            value = current - (image - con[at(k), :] * here)
            value = jnp.where((row >= 0) & (row < n * rows), value, 0.0)
            v0[at(k), :] = value
            return summed_up(k, sums, (value * value,))

        low, high = HALO // TILE + 1, tiles - HALO // TILE - 1
        plan = ((weights, low, high), (edges, low + 1, high - 1), (residual, low + 1, high - 1))
        sums = zeros(1)
        for work, begin, end in plan:
            sums = lax.fori_loop(begin, end, work, sums, unroll=end - begin)
        arrived()
        for work, begin, end in plan:
            for k in (*range(begin), *range(end, tiles)):
                sums = work(k, sums)
        (m0,) = sums

        def power_1(k, sums):
            here, image = apply(v0, k)
            v1[at(k), :] = image
            return summed_up(k, sums, (here * image, image * image))

        m1, m2 = lax.fori_loop(0, tiles, power_1, zeros(2), unroll=tiles)

        def power_2(k, sums):
            here, image = apply(v1, k)
            v2[at(k), :] = image
            return summed_up(k, sums, (here * image,))

        (m3,) = lax.fori_loop(0, tiles, power_2, zeros(1), unroll=tiles)
        shared(2 * sweep, (m0, m1, m2, m3))

        @pl.loop(0, tiles, unroll=tiles)
        def _(k):
            v3[at(k), :] = apply(v2, k)[1]

        @pl.loop(0, tiles, unroll=tiles)
        def _(k):
            v4[at(k), :] = apply(v3, k)[1]

        m0, m1, m2, m3 = gathered(2 * sweep, 4)
        a0 = m0 / m1
        rr1 = a0 * a0 * m2 - m0
        b0 = rr1 / m0
        g0 = 1.0 + b0
        pmp = g0 * g0 * m1 - 2.0 * g0 * a0 * m2 + a0 * a0 * m3
        a1 = rr1 / pmp
        ca = a0 + a1 * g0
        cb = a0 * a1

        def combine(k, sums):
            x1, x2, x3 = v1[at(k), :], v2[at(k), :], v3[at(k), :]
            r0 = v0[at(k), :] - ca * x1 + cb * x2
            r1 = x1 - ca * x2 + cb * x3
            r2 = x2 - ca * x3 + cb * v4[at(k), :]
            v2[at(k), :] = r0
            v3[at(k), :] = r1
            v4[at(k), :] = r2
            return summed_up(k, sums, (r0 * r0, r0 * r1, r1 * r1, r1 * r2, r2 * r2))

        h = lax.fori_loop(0, tiles, combine, zeros(5), unroll=tiles)

        def power_5(k, sums):
            here, image = apply(v4, k)
            return (sums[0] + folded(here * image),)

        (h5,) = lax.fori_loop(
            HALO // TILE, tiles - HALO // TILE, power_5, zeros(1), unroll=rows // TILE)
        shared(2 * sweep + 1, h + (h5,))
        idle()
        h0, h1, h2, h3, h4, h5 = gathered(2 * sweep + 1, 6)
        i0, i1 = 1.0 / a0, 1.0 / a1
        mix = i1 + b0 * i0
        q0 = -h0 * i1
        q1 = (q0 - h1) * i1
        q2 = (mix * q0 - h1 * i1 - h2) * i1
        f1 = -q0 * i0
        f2 = (-q0 * i0 + h1 * i1 - mix * q0) * i0
        ip, i_m = 1.0 / pmp, 1.0 / m1
        s00 = h1 - q0 * q0 * ip
        s01 = h2 - q0 * q1 * ip
        s02 = h3 - q0 * q2 * ip
        s11 = h3 - q1 * q1 * ip - f1 * f1 * i_m
        s12 = h4 - q1 * q2 * ip - f1 * f2 * i_m
        s22 = h5 - q2 * q2 * ip - f2 * f2 * i_m
        l10, l20 = s01 / s00, s02 / s00
        d1 = s11 - l10 * s01
        e12 = s12 - l10 * s02
        z1 = h1 - l10 * h0
        usable1 = d1 > TINY * h3
        l21 = jnp.where(usable1, e12 / d1, 0.0)
        d2 = s22 - l20 * s02 - l21 * e12
        z2 = h2 - l20 * h0 - l21 * z1
        y2 = jnp.where(usable1 & (d2 > TINY * h5), z2 / d2, 0.0)
        y1 = jnp.where(usable1, z1 / d1, 0.0) - l21 * y2
        y0 = h0 / s00 - l10 * y1 - l20 * y2
        c1 = -(y0 * q0 + y1 * q1 + y2 * q2) * ip
        c0 = -(y1 * f1 + y2 * f2) * i_m
        e0 = ca + c0 + c1 * g0
        e1 = -cb - c1 * a0

        def result(k):
            return (
                field[at(k), :] + (e0 * v0[at(k), :] + e1 * v1[at(k), :])
                + (y0 * v2[at(k), :] + y1 * v3[at(k), :] + y2 * v4[at(k), :])
            )

        finish(result)

    inside = (HALO // TILE, tiles - HALO // TILE)

    def between(result):
        u1[at(inside[0]), :] = result(inside[0])
        start_up(halo_next)
        u1[at(inside[1] - 1), :] = result(inside[1] - 1)
        start_down(halo_next)

        @pl.loop(inside[0] + 1, inside[1] - 1, unroll=inside[1] - inside[0] - 2)
        def _(k):
            u1[at(k), :] = result(k)

    span = rows // CHUNKS
    onward = [
        pltpu.make_async_remote_copy(
            src_ref=out_ref.at[0, pl.ds(c * span, span)], dst_ref=carry.at[pl.ds(c * span, span)],
            send_sem=send_c.at[c], recv_sem=recv_c.at[c], device_id={"tm": t + 1}, device_id_type=MESH)
        for c in range(CHUNKS)
    ]

    def decays():
        sent(halo_next)

        @pl.when(t > 0)
        def _():
            @pl.loop(0, rows // TILE, unroll=rows // TILE)
            def _(k):
                up = k + HALO // TILE
                conduct = con[at(up), :]
                decay = conduct / (conduct + LUMPED * base[at(up), :])
                wgt[at(k), :] = decay
                u1[at(up), :] = u1[at(up), :] - decay * u0[at(up), :]

    def final(result):
        @pl.when(t > 0)
        def _():
            @pl.loop(0, rows // TILE, unroll=rows // TILE)
            def _(k):
                out_ref[0, at(k), :] = result(k + HALO // TILE)

        for c in range(CHUNKS):
            @pl.when(t == 0)
            def _():
                @pl.loop(c * span // TILE, (c + 1) * span // TILE, unroll=span // TILE)
                def _(k):
                    out_ref[0, at(k), :] = result(k + HALO // TILE)

            @pl.when(t > 0)
            def _():
                onward[c].wait_recv()

                @pl.loop(c * span // TILE, (c + 1) * span // TILE, unroll=span // TILE)
                def _(k):
                    out_ref[0, at(k), :] = out_ref[0, at(k), :] + wgt[at(k), :] * carry[at(k), :]

            @pl.when(t < slices - 1)
            def _():
                onward[c].start()

    fine_step(0, u0, first_halos, lambda: None, between)
    fine_step(1, u1, later_halos, decays, final)

    for pair in (halo_reg, halo_src, halo_first):
        sent(pair)

    @pl.when(t < slices - 1)
    def _():
        for copy in pieces + onward:
            copy.wait_send()

    for slot in range(2 * FSTEPS):
        everyone(slot, send_s).wait()


def shards(slices, n, prev_ends, initial, source, region, conductivity, reluctivity, saturation):
    rows, cols = initial.shape
    tall = rows + 2 * HALO
    grid = pltpu.VMEM((tall, cols), jnp.float32)
    hbm = pl.BlockSpec(memory_space=pltpu.HBM)
    dma = pltpu.SemaphoreType.DMA
    return pl.pallas_call(
        functools.partial(kernel, slices, n),
        out_shape=jax.ShapeDtypeStruct((1, rows, cols), jnp.float32),
        in_specs=[hbm] * 7,
        out_specs=pl.BlockSpec(memory_space=pltpu.VMEM),
        scratch_shapes=[
            grid, grid, pltpu.VMEM((tall, cols), jnp.int32), pltpu.VMEM((2, tall, cols), jnp.float32),
            *([grid] * 14),
            pltpu.VMEM((rows, cols), jnp.float32),
            pltpu.VMEM((2 * FSTEPS, n, TILE, LANES), jnp.float32),
            *([pltpu.SMEM((REGIONS,), jnp.float32)] * 3),
            dma((6,)), dma((8,)), dma((8,)), dma((3,)), dma((3,)), dma((CHUNKS,)), dma((CHUNKS,)),
            dma((2 * FSTEPS,)), dma((2 * FSTEPS,)),
        ],
        compiler_params=pltpu.CompilerParams(
            collective_id=0, has_side_effects=True, vmem_limit_bytes=63 * 1024 * 1024),
    )(prev_ends, initial, source, region, conductivity, reluctivity, saturation)


def solution(mesh):
    in_specs = (
        P("tm", "mesh", None), P("mesh", None), P(None, "mesh", None), P("mesh", None), P(), P(), P(),
    )
    return jax.shard_map(
        functools.partial(shards, mesh.shape["tm"], mesh.shape["mesh"]),
        mesh=mesh, in_specs=in_specs, out_specs=P("tm", "mesh", None), check_vma=False)
```

```python
import functools

import jax
import jax.numpy as jnp
from jax import lax
from jax.experimental import pallas as pl
from jax.experimental.pallas import tpu as pltpu
from jax.sharding import PartitionSpec as P

FSTEPS = 2
REGIONS = 4
STEP_LENGTH = 1.0
FREQUENCY = 0.1
LUMPED = 0.02
TILE = 8
HALO = 8
LANES = 128
CHUNKS = 4
MESH = pl.DeviceIdType.MESH
TINY = 3e-7


def folded(product):
    total = product[:, 0:LANES]
    for cut in range(1, product.shape[1] // LANES):
        total = total + product[:, cut * LANES : (cut + 1) * LANES]
    return total


def kernel(
    slices, n,
    prev_ref, initial_ref, source_ref, region_ref, con_ref, rel_ref, sat_ref,
    out_ref,
    stage, u0, u1, reg, src, con, base, slope, wgt, diag, w_s, w_n, w_e, w_w,
    v0, v1, v2, v3, v4, carry, parts, con_tab, rel_tab, sat_tab,
    local_sem, send_h, recv_h, send_p, recv_p, send_c, recv_c, send_s, recv_s,
):
    t = lax.axis_index("tm")
    m = lax.axis_index("mesh")
    rows, cols = initial_ref.shape
    tall = rows + 2 * HALO
    tiles = tall // TILE
    first, last = m == 0, m == n - 1
    inner = pl.ds(HALO, rows)

    loads = [
        pltpu.make_async_copy(region_ref, reg.at[inner], local_sem.at[0]),
        pltpu.make_async_copy(source_ref, src.at[:, inner], local_sem.at[1]),
        pltpu.make_async_copy(con_ref, con_tab, local_sem.at[3]),
        pltpu.make_async_copy(rel_ref, rel_tab, local_sem.at[4]),
        pltpu.make_async_copy(sat_ref, sat_tab, local_sem.at[5]),
    ]
    load_start = pltpu.make_async_copy(initial_ref, u0.at[inner], local_sem.at[2])
    for copy in loads:
        copy.start()

    @pl.when(t == 0)
    def _():
        load_start.start()

    barrier = pltpu.get_barrier_semaphore()
    for hop in range(1, n):
        pl.semaphore_signal(barrier, inc=1, device_id={"mesh": lax.rem(m + hop, n)}, device_id_type=MESH)

    @pl.when(t > 0)
    def _():
        pl.semaphore_signal(barrier, inc=1, device_id={"tm": t - 1}, device_id_type=MESH)

    @pl.when(t < slices - 1)
    def _():
        pl.semaphore_signal(barrier, inc=1, device_id={"tm": t + 1}, device_id_type=MESH)

    def blank(at):
        u0[at, :] = jnp.zeros((HALO, cols), jnp.float32)
        u1[at, :] = jnp.zeros((HALO, cols), jnp.float32)
        src[:, at, :] = jnp.zeros((2, HALO, cols), jnp.float32)
        reg[at, :] = jnp.full((HALO, cols), REGIONS, jnp.int32)

    top, bottom = pl.ds(0, HALO), pl.ds(HALO + rows, HALO)

    @pl.when(first)
    def _():
        blank(top)

    @pl.when(last)
    def _():
        blank(bottom)

    middle = (t > 0) & (t < slices - 1)

    @pl.when(middle)
    def _():
        pl.semaphore_wait(barrier, n + 1)

    @pl.when(jnp.logical_not(middle))
    def _():
        pl.semaphore_wait(barrier, n - 1 + min(slices - 1, 1))

    low, high = pl.ds(0, HALO), pl.ds(rows - HALO, HALO)
    own_low, own_high = pl.ds(HALO, HALO), pl.ds(rows, HALO)

    def halo(slot, up_src, up_dst, down_src, down_dst):
        up = pltpu.make_async_remote_copy(
            src_ref=up_src, dst_ref=up_dst, send_sem=send_h.at[2 * slot], recv_sem=recv_h.at[2 * slot],
            device_id={"mesh": m - 1}, device_id_type=MESH)
        down = pltpu.make_async_remote_copy(
            src_ref=down_src, dst_ref=down_dst, send_sem=send_h.at[2 * slot + 1], recv_sem=recv_h.at[2 * slot + 1],
            device_id={"mesh": m + 1}, device_id_type=MESH)
        return up, down

    halo_reg = halo(0, region_ref.at[low], reg.at[bottom], region_ref.at[high], reg.at[top])
    halo_src = halo(1, source_ref.at[:, low], src.at[:, bottom], source_ref.at[:, high], src.at[:, top])
    halo_first = halo(2, initial_ref.at[low], u0.at[bottom], initial_ref.at[high], u0.at[top])
    halo_later = halo(2, u0.at[own_low], u0.at[bottom], u0.at[own_high], u0.at[top])
    halo_next = halo(3, u1.at[own_low], u1.at[bottom], u1.at[own_high], u1.at[top])

    def start_up(pair):
        @pl.when(m > 0)
        def _():
            pair[0].start()

    def start_down(pair):
        @pl.when(m < n - 1)
        def _():
            pair[1].start()

    def arrive(pair):
        @pl.when(m < n - 1)
        def _():
            pair[0].wait_recv()

        @pl.when(m > 0)
        def _():
            pair[1].wait_recv()

    def sent(pair):
        @pl.when(m > 0)
        def _():
            pair[0].wait_send()

        @pl.when(m < n - 1)
        def _():
            pair[1].wait_send()

    pieces = []
    for k, (offset, length) in enumerate(((0, HALO), (rows - HALO, HALO), (HALO, rows - 2 * HALO))):
        pieces.append(pltpu.make_async_remote_copy(
            src_ref=prev_ref.at[0, pl.ds(offset, length)], dst_ref=u0.at[pl.ds(HALO + offset, length)],
            send_sem=send_p.at[k], recv_sem=recv_p.at[k], device_id={"tm": t + 1}, device_id_type=MESH))

    @pl.when(t < slices - 1)
    def _():
        for piece in pieces:
            piece.start()

    @pl.when(t == 0)
    def _():
        start_up(halo_first)
        start_down(halo_first)

    for pair in (halo_reg, halo_src):
        start_up(pair)
        start_down(pair)

    @pl.when(t > 0)
    def _():
        pieces[0].wait_recv()
        start_up(halo_later)
        pieces[1].wait_recv()
        start_down(halo_later)

    def at(k):
        return pl.ds(pl.multiple_of(k * TILE, TILE), TILE)

    sub = lax.broadcasted_iota(jnp.int32, (TILE, cols), 0)
    lane = lax.broadcasted_iota(jnp.int32, (TILE, cols), 1)

    def around(ref, k):
        here = ref[at(k), :]
        before = ref[at(lax.rem(k + tiles - 1, tiles)), :]
        after = ref[at(lax.rem(k + 1, tiles)), :]
        south = pltpu.roll(jnp.where(sub == 0, after, here), TILE - 1, 0)
        north = pltpu.roll(jnp.where(sub == TILE - 1, before, here), 1, 0)
        east = pltpu.roll(here, cols - 1, 1)
        west = pltpu.roll(here, 1, 1)
        return here, south, north, east, west

    def apply(ref, k):
        here, south, north, east, west = around(ref, k)
        image = (
            diag[at(k), :] * here
            - (w_s[at(k), :] * south + w_n[at(k), :] * north)
            - (w_e[at(k), :] * east + w_w[at(k), :] * west)
        )
        return here, image

    loads[0].wait()
    for copy in loads[2:]:
        copy.wait()
    arrive(halo_reg)

    @pl.loop(0, tiles, unroll=tiles)
    def _(k):
        kind = reg[at(k), :]
        for table, into in ((con_tab, con), (rel_tab, base), (sat_tab, slope)):
            value = jnp.zeros((TILE, cols), jnp.float32)
            for material in range(REGIONS):
                value = jnp.where(kind == material, table[material], value)
            into[at(k), :] = value

    loads[1].wait()

    @pl.when(t == 0)
    def _():
        load_start.wait()

    @pl.when(t > 0)
    def _():
        pieces[2].wait_recv()

    def first_halos():
        arrive(halo_src)
        arrive(halo_first)

    def later_halos():
        arrive(halo_next)

    def shared(slot, sums):
        for k, partial in enumerate(sums):
            parts[slot, m, k : k + 1, :] = jnp.sum(partial, axis=0, keepdims=True)
        for k in range(len(sums), TILE):
            parts[slot, m, k : k + 1, :] = jnp.zeros((1, LANES), jnp.float32)
        for hop in sorted(range(1, n), key=lambda h: -min(h, n - h)):
            pltpu.make_async_remote_copy(
                src_ref=parts.at[slot, m], dst_ref=parts.at[slot, m],
                send_sem=send_s.at[slot], recv_sem=recv_s.at[slot],
                device_id={"mesh": lax.rem(m + hop, n)}, device_id_type=MESH).start()

    def everyone(slot, sem):
        return pltpu.make_async_copy(
            parts.at[slot, pl.ds(0, n - 1)], parts.at[slot, pl.ds(0, n - 1)], sem.at[slot])

    def gathered(slot, count):
        everyone(slot, recv_s).wait()
        total = parts[slot, 0]
        for other in range(1, n):
            total = total + parts[slot, other]
        summed = jnp.sum(total, axis=1, keepdims=True)
        return [summed[k : k + 1, :] for k in range(count)]

    def owned(k):
        return (k >= HALO // TILE) & (k < tiles - HALO // TILE)

    def zeros(count):
        return tuple(jnp.zeros((TILE, LANES), jnp.float32) for _ in range(count))

    def summed_up(k, sums, products):
        keep = jnp.where(owned(k), 1.0, 0.0)
        return tuple(s + keep * folded(p) for s, p in zip(sums, products))

    def fine_step(sweep, field, arrived, idle, finish):
        moment = (t.astype(jnp.float32) * FSTEPS + sweep + 1) * STEP_LENGTH
        angle = jnp.full((1, 1), FREQUENCY * moment, jnp.float32)
        cosine, sine = jnp.cos(angle), jnp.sin(angle)

        def weights(k, sums):
            here, south, north, east, west = around(field, k)
            east = jnp.where(lane == cols - 1, 0.0, east)
            west = jnp.where(lane == 0, 0.0, west)
            grad_x = 0.5 * (south - north)
            grad_y = 0.5 * (east - west)
            wgt[at(k), :] = base[at(k), :] * (1.0 + slope[at(k), :] * (grad_x * grad_x + grad_y * grad_y))
            return sums

        def edges(k, sums):
            here, south, north, east, west = around(wgt, k)
            east = 0.5 * (here + jnp.where(lane == cols - 1, 0.0, east))
            west = 0.5 * (here + jnp.where(lane == 0, 0.0, west))
            south = 0.5 * (here + south)
            north = 0.5 * (here + north)
            conduct = con[at(k), :]
            diag[at(k), :] = conduct + (south + north) + (east + west)
            row = m * rows + k * TILE - HALO + sub
            w_s[at(k), :] = jnp.where((row >= 0) & (row < n * rows - 1), south, 0.0)
            w_n[at(k), :] = jnp.where((row >= 1) & (row < n * rows), north, 0.0)
            w_e[at(k), :] = jnp.where(lane == cols - 1, 0.0, east)
            w_w[at(k), :] = jnp.where(lane == 0, 0.0, west)
            return sums

        def residual(k, sums):
            here, image = apply(field, k)
            current = src[0, at(k), :] * cosine + src[1, at(k), :] * sine
            row = m * rows + k * TILE - HALO + sub
            value = current - (image - con[at(k), :] * here)
            value = jnp.where((row >= 0) & (row < n * rows), value, 0.0)
            v0[at(k), :] = value
            return summed_up(k, sums, (value * value,))

        low, high = HALO // TILE + 1, tiles - HALO // TILE - 1
        plan = ((weights, low, high), (edges, low + 1, high - 1), (residual, low + 1, high - 1))
        sums = zeros(1)
        for work, begin, end in plan:
            sums = lax.fori_loop(begin, end, work, sums, unroll=end - begin)
        arrived()
        for work, begin, end in plan:
            for k in (*range(begin), *range(end, tiles)):
                sums = work(k, sums)
        (m0,) = sums

        def power_1(k, sums):
            here, image = apply(v0, k)
            v1[at(k), :] = image
            return summed_up(k, sums, (here * image, image * image))

        m1, m2 = lax.fori_loop(0, tiles, power_1, zeros(2), unroll=tiles)

        def power_2(k, sums):
            here, image = apply(v1, k)
            v2[at(k), :] = image
            return summed_up(k, sums, (here * image,))

        (m3,) = lax.fori_loop(0, tiles, power_2, zeros(1), unroll=tiles)
        shared(2 * sweep, (m0, m1, m2, m3))

        @pl.loop(0, tiles, unroll=tiles)
        def _(k):
            v3[at(k), :] = apply(v2, k)[1]

        @pl.loop(0, tiles, unroll=tiles)
        def _(k):
            v4[at(k), :] = apply(v3, k)[1]

        m0, m1, m2, m3 = gathered(2 * sweep, 4)
        a0 = m0 / m1
        rr1 = a0 * a0 * m2 - m0
        b0 = rr1 / m0
        g0 = 1.0 + b0
        pmp = g0 * g0 * m1 - 2.0 * g0 * a0 * m2 + a0 * a0 * m3
        a1 = rr1 / pmp
        ca = a0 + a1 * g0
        cb = a0 * a1

        def combine(k, sums):
            x1, x2, x3 = v1[at(k), :], v2[at(k), :], v3[at(k), :]
            r0 = v0[at(k), :] - ca * x1 + cb * x2
            r1 = x1 - ca * x2 + cb * x3
            r2 = x2 - ca * x3 + cb * v4[at(k), :]
            v2[at(k), :] = r0
            v3[at(k), :] = r1
            v4[at(k), :] = r2
            return summed_up(k, sums, (r0 * r0, r0 * r1, r1 * r1, r1 * r2, r2 * r2))

        h = lax.fori_loop(0, tiles, combine, zeros(5), unroll=tiles)

        def power_5(k, sums):
            here, image = apply(v4, k)
            return (sums[0] + folded(here * image),)

        (h5,) = lax.fori_loop(
            HALO // TILE, tiles - HALO // TILE, power_5, zeros(1), unroll=rows // TILE)
        shared(2 * sweep + 1, h + (h5,))
        idle()
        h0, h1, h2, h3, h4, h5 = gathered(2 * sweep + 1, 6)
        i0, i1 = 1.0 / a0, 1.0 / a1
        mix = i1 + b0 * i0
        q0 = -h0 * i1
        q1 = (q0 - h1) * i1
        q2 = (mix * q0 - h1 * i1 - h2) * i1
        f1 = -q0 * i0
        f2 = (-q0 * i0 + h1 * i1 - mix * q0) * i0
        ip, i_m = 1.0 / pmp, 1.0 / m1
        s00 = h1 - q0 * q0 * ip
        s01 = h2 - q0 * q1 * ip
        s02 = h3 - q0 * q2 * ip
        s11 = h3 - q1 * q1 * ip - f1 * f1 * i_m
        s12 = h4 - q1 * q2 * ip - f1 * f2 * i_m
        s22 = h5 - q2 * q2 * ip - f2 * f2 * i_m
        l10, l20 = s01 / s00, s02 / s00
        d1 = s11 - l10 * s01
        e12 = s12 - l10 * s02
        z1 = h1 - l10 * h0
        usable1 = d1 > TINY * h3
        l21 = jnp.where(usable1, e12 / d1, 0.0)
        d2 = s22 - l20 * s02 - l21 * e12
        z2 = h2 - l20 * h0 - l21 * z1
        y2 = jnp.where(usable1 & (d2 > TINY * h5), z2 / d2, 0.0)
        y1 = jnp.where(usable1, z1 / d1, 0.0) - l21 * y2
        y0 = h0 / s00 - l10 * y1 - l20 * y2
        c1 = -(y0 * q0 + y1 * q1 + y2 * q2) * ip
        c0 = -(y1 * f1 + y2 * f2) * i_m
        e0 = ca + c0 + c1 * g0
        e1 = -cb - c1 * a0

        def result(k):
            return (
                field[at(k), :] + (e0 * v0[at(k), :] + e1 * v1[at(k), :])
                + (y0 * v2[at(k), :] + y1 * v3[at(k), :] + y2 * v4[at(k), :])
            )

        finish(result)

    inside = (HALO // TILE, tiles - HALO // TILE)

    def between(result):
        u1[at(inside[0]), :] = result(inside[0])
        start_up(halo_next)
        u1[at(inside[1] - 1), :] = result(inside[1] - 1)
        start_down(halo_next)

        @pl.loop(inside[0] + 1, inside[1] - 1, unroll=inside[1] - inside[0] - 2)
        def _(k):
            u1[at(k), :] = result(k)

    span = rows // CHUNKS
    onward = [
        pltpu.make_async_remote_copy(
            src_ref=stage.at[0, pl.ds(c * span, span)], dst_ref=carry.at[pl.ds(c * span, span)],
            send_sem=send_c.at[c], recv_sem=recv_c.at[c], device_id={"tm": t + 1}, device_id_type=MESH)
        for c in range(CHUNKS)
    ]

    stores = [
        pltpu.make_async_copy(
            stage.at[0, pl.ds(c * span, span)], out_ref.at[0, pl.ds(c * span, span)], local_sem.at[6 + c])
        for c in range(CHUNKS)
    ]

    def decays():
        sent(halo_next)

        @pl.when(t > 0)
        def _():
            @pl.loop(0, rows // TILE, unroll=rows // TILE)
            def _(k):
                up = k + HALO // TILE
                conduct = con[at(up), :]
                decay = conduct / (conduct + LUMPED * base[at(up), :])
                wgt[at(k), :] = decay
                u1[at(up), :] = u1[at(up), :] - decay * u0[at(up), :]

    def final(result):
        @pl.when(t > 0)
        def _():
            @pl.loop(0, rows // TILE, unroll=rows // TILE)
            def _(k):
                stage[0, at(k), :] = result(k + HALO // TILE)

        for c in range(CHUNKS):
            @pl.when(t == 0)
            def _():
                @pl.loop(c * span // TILE, (c + 1) * span // TILE, unroll=span // TILE)
                def _(k):
                    stage[0, at(k), :] = result(k + HALO // TILE)

            @pl.when(t > 0)
            def _():
                onward[c].wait_recv()

                @pl.loop(c * span // TILE, (c + 1) * span // TILE, unroll=span // TILE)
                def _(k):
                    stage[0, at(k), :] = stage[0, at(k), :] + wgt[at(k), :] * carry[at(k), :]

            @pl.when(t < slices - 1)
            def _():
                onward[c].start()

            stores[c].start()

    fine_step(0, u0, first_halos, lambda: None, between)
    fine_step(1, u1, later_halos, decays, final)

    for pair in (halo_reg, halo_src, halo_first):
        sent(pair)

    @pl.when(t < slices - 1)
    def _():
        for copy in pieces + onward:
            copy.wait_send()

    for store in stores:
        store.wait()

    for slot in range(2 * FSTEPS):
        everyone(slot, send_s).wait()


def shards(slices, n, prev_ends, initial, source, region, conductivity, reluctivity, saturation):
    rows, cols = initial.shape
    tall = rows + 2 * HALO
    grid = pltpu.VMEM((tall, cols), jnp.float32)
    hbm = pl.BlockSpec(memory_space=pltpu.HBM)
    dma = pltpu.SemaphoreType.DMA
    return pl.pallas_call(
        functools.partial(kernel, slices, n),
        out_shape=jax.ShapeDtypeStruct((1, rows, cols), jnp.float32),
        in_specs=[hbm] * 7,
        out_specs=hbm,
        scratch_shapes=[
            pltpu.VMEM((1, rows, cols), jnp.float32), grid, grid, pltpu.VMEM((tall, cols), jnp.int32), pltpu.VMEM((2, tall, cols), jnp.float32),
            *([grid] * 14),
            pltpu.VMEM((rows, cols), jnp.float32),
            pltpu.VMEM((2 * FSTEPS, n, TILE, LANES), jnp.float32),
            *([pltpu.SMEM((REGIONS,), jnp.float32)] * 3),
            dma((6 + CHUNKS,)), dma((8,)), dma((8,)), dma((3,)), dma((3,)), dma((CHUNKS,)), dma((CHUNKS,)),
            dma((2 * FSTEPS,)), dma((2 * FSTEPS,)),
        ],
        compiler_params=pltpu.CompilerParams(
            collective_id=0, has_side_effects=True, vmem_limit_bytes=63 * 1024 * 1024),
    )(prev_ends, initial, source, region, conductivity, reluctivity, saturation)


def solution(mesh):
    in_specs = (
        P("tm", "mesh", None), P("mesh", None), P(None, "mesh", None), P("mesh", None), P(), P(), P(),
    )
    return jax.shard_map(
        functools.partial(shards, mesh.shape["tm"], mesh.shape["mesh"]),
        mesh=mesh, in_specs=in_specs, out_specs=P("tm", "mesh", None), check_vma=False)
```
